32 devices in a mesh: groups: 1, gx: 8 (over y, x, core), gy: 4 (over z).
Axes of the slice: x: 2, y: 2, z: 4, core: 2. Of those that a mesh axis runs over, the one named last changes fastest.
Arguments:
- tokens: bfloat16 [256, 8192], P(('groups', 'gx'), 'gy'), may hold values from -6 to 6
- w_gate: bfloat16 [8192, 64, 128], P('gy', 'gx'), may hold values from -0.0625 to 0.0625
- w_x: bfloat16 [8192, 64, 128], P('gy', 'gx'), may hold values from -0.0625 to 0.0625
- w_bc: bfloat16 [8192, 256], P('gy'), may hold values from -0.005859375 to 0.005859375
- w_dt: bfloat16 [8192, 64], P('gy', 'gx'), may hold values from -0.0625 to 0.0625
- conv_x_w: float32 [4, 64, 128], P(None, 'gx', 'gy'), may hold values from -3 to 3
- conv_bc_w: float32 [4, 256], replicated, may hold values from -3 to 3
- conv_x_state: float32 [3, 64, 128], P(None, ('groups', 'gx'), 'gy'), may hold values from -6 to 6
- conv_bc_state: float32 [3, 256], P(None, 'groups'), may hold values from -0.6 to 0.6
- dt_bias: float32 [64], P('gx'), may hold values from -1 to 1
- decay_rate: float32 [64], P('gx'), may hold values from 0.0003 to 0.1
- skip_d: float32 [64], P('gx'), may hold values from 0.5 to 1.5
- state_in: float32 [64, 128, 128], P(('groups', 'gx'), 'gy'), may hold values from -18 to 18
- norm_gain: float32 [64, 128], P('gx'), may hold values from 0.5 to 1.5
- w_out: bfloat16 [64, 128, 8192], P('gx', None, 'gy'), may hold values from -0.0625 to 0.0625
Outputs:
- mixed_out: bfloat16 [256, 8192], P(('groups', 'gx'), 'gy')
- state_out: float32 [64, 128, 128], P(('groups', 'gx'), 'gy')
The draws below stay inside these ranges and needn't reach their ends.
All inputs are finite; a program needn't handle non-finite values.
Results may differ from the reference program's by a relative error of at most 0.02.
Values may be sent and summed in bfloat16 or wider, within the bound.
A program may use at most 64 MiB of HBM per device.

```python
import math
import jax
import jax.numpy as jnp
from jax import lax

D = 8192
HEADS = 64
HEAD_DIM = 128
STATE = 128
CONV = 4
SSD_BLOCK = 256
TOKENS = 256
INNER = 8192
N_GY = 4


def shard_levels(own_key, extent, cuts, smallest, top_value):
    def one(position, blocks):
        draws = jax.random.uniform(jax.random.fold_in(jax.random.fold_in(own_key, 6), position), (blocks,), jnp.float32, smallest / len(cuts), top_value / len(cuts))
        return jnp.repeat(jnp.exp(draws), extent[position] // blocks).reshape((-1,) + (1,) * (len(extent) - position - 1))

    loudness = one(*cuts[0])
    for cut in cuts[1:]:
        loudness = loudness * one(*cut)
    return loudness


def bell_draw(stream_key, dims, scale, bound, cuts=(), held_as=jnp.bfloat16):
    values = scale * jax.random.normal(stream_key, dims, jnp.float32)
    if cuts:
        values = values * shard_levels(stream_key, dims, cuts, -0.22, 0.18)
    return jnp.clip(values, -bound, bound).astype(held_as)


def setup_inputs(seed: int = 0, part: int = 0) -> dict:
    streams_of = jax.random.split(jax.random.key(seed), 16)
    part_splits = jax.random.split(jax.random.fold_in(streams_of[15], part), 16)
    return {
        "tokens": bell_draw(part_splits[0], (TOKENS, D), 1.0, 6.0, ((0, 8), (1, 4))),
        "w_gate": bell_draw(streams_of[1], (D, HEADS, HEAD_DIM), D ** -0.5, 0.0625, ((0, 4), (1, 8))),
        "w_x": bell_draw(streams_of[2], (D, HEADS, HEAD_DIM), D ** -0.5, 0.0625, ((0, 4), (1, 8))),
        "w_bc": bell_draw(streams_of[3], (D, 2 * STATE), (D * STATE) ** -0.5, 0.005859375, ((0, 4),)),
        "w_dt": bell_draw(streams_of[4], (D, HEADS), D ** -0.5, 0.0625, ((0, 4), (1, 8))),
        "conv_x_w": bell_draw(streams_of[5], (CONV, HEADS, HEAD_DIM), 0.5, 3.0, ((1, 8), (2, 4)), jnp.float32),
        "conv_bc_w": bell_draw(streams_of[6], (CONV, 2 * STATE), 0.5, 3.0, (), jnp.float32),
        "conv_x_state": bell_draw(part_splits[7], (CONV - 1, HEADS, HEAD_DIM), 1.0, 6.0, ((1, 8), (2, 4)), jnp.float32),
        "conv_bc_state": bell_draw(part_splits[8], (CONV - 1, 2 * STATE), 0.1, 0.6, (), jnp.float32),
        "dt_bias": jnp.clip(jax.random.uniform(streams_of[9], (HEADS,), jnp.float32, -1.0, 1.0) * shard_levels(streams_of[9], (HEADS,), ((0, 8),), -0.4, 0.0), -1.0, 1.0),
        "decay_rate": jnp.clip(jnp.exp(math.log(0.1) - 5.809143 * jax.random.uniform(streams_of[10], (HEADS,), jnp.float32) ** shard_levels(streams_of[10], (HEADS,), ((0, 8),), -0.2, 0.2)), 0.0003, 0.1),
        "skip_d": jnp.clip(0.5 + 1.0 * jax.random.uniform(streams_of[11], (HEADS,), jnp.float32) ** shard_levels(streams_of[11], (HEADS,), ((0, 8),), -0.2, 0.2), 0.5, 1.5),
        "state_in": bell_draw(part_splits[12], (HEADS, HEAD_DIM, STATE), 3.0, 18.0, ((0, 8), (1, 4)), jnp.float32),
        "norm_gain": jnp.clip(1.0 + 0.1 * jax.random.normal(streams_of[13], (HEADS, HEAD_DIM), jnp.float32), 0.5, 1.5),
        "w_out": bell_draw(streams_of[14], (HEADS, HEAD_DIM, D), INNER ** -0.5, 0.0625, ((0, 8), (2, 4))),
    }


def conv_silu(pre, carried, taps):
    padded = jnp.concatenate([carried, pre], axis=0)
    length = pre.shape[0]
    acc = jnp.zeros(pre.shape, jnp.float32)
    for index in range(taps.shape[0]):
        acc = acc + taps[index] * padded[index:index + length]
    return jax.nn.silu(acc)

def ssd_blocks(values, b_mat, c_mat, delta, log_decay, state, block):
    total, heads, width = values.shape
    count = total // block
    states = b_mat.shape[1]
    lower = jnp.arange(block)[:, None] >= jnp.arange(block)[None, :]
    high = lax.Precision.HIGHEST

    def advance(carry, inputs):
        vals, bm, cm, dl, ld = inputs
        cum = jnp.cumsum(ld, axis=0)
        scores = jnp.dot(cm, bm.T, precision=high)
        gap = cum.T[:, :, None] - cum.T[:, None, :]
        decay = jnp.exp(jnp.where(lower[None], gap, -jnp.inf))
        weights = decay * scores[None]
        scaled = vals * dl[:, :, None]
        inner = jnp.einsum('hts,shp->thp', weights, scaled, precision=high)
        carried = jnp.exp(cum)[:, :, None] * jnp.einsum('tn,hpn->thp', cm, carry, precision=high)
        tail = jnp.exp(cum[-1][None, :] - cum)
        update = jnp.einsum('sh,shp,sn->hpn', tail, scaled, bm, precision=high)
        new_state = jnp.exp(cum[-1])[:, None, None] * carry + update
        return (new_state, inner + carried)
    inputs = (values.reshape(count, block, heads, width), b_mat.reshape(count, block, states), c_mat.reshape(count, block, states), delta.reshape(count, block, heads), log_decay.reshape(count, block, heads))
    final, outputs = lax.scan(advance, state, inputs)
    return (outputs.reshape(total, heads, width), final)

def rounded_partials(tokens, weight, parts):
    rows = tokens.shape[1] // parts

    def add_block(index, acc):
        start = (index * rows).astype(jnp.int32)
        left = lax.dynamic_slice_in_dim(tokens, start, rows, 1)
        right = lax.dynamic_slice_in_dim(weight, start, rows, 0)
        partial_value = jnp.dot(left, right, preferred_element_type=jnp.float32).astype(jnp.bfloat16)
        partial_value = lax.optimization_barrier(partial_value)
        return acc + partial_value.astype(jnp.float32)
    empty = jnp.zeros((tokens.shape[0], weight.shape[1]), jnp.float32)
    return lax.fori_loop(jnp.int32(0), jnp.int32(parts), add_block, empty)

def reference(tokens, w_gate, w_x, w_bc, w_dt, conv_x_w, conv_bc_w, conv_x_state, conv_bc_state, dt_bias, decay_rate, skip_d, state_in, norm_gain, w_out):
    total = tokens.shape[0]
    model = tokens.shape[1]
    heads, width = (w_gate.shape[1], w_gate.shape[2])
    gate_pre = rounded_partials(tokens, w_gate.reshape(model, heads * width), N_GY).reshape(total, heads, width)
    x_pre = rounded_partials(tokens, w_x.reshape(model, heads * width), N_GY).reshape(total, heads, width)
    bc_pre = jnp.dot(tokens, w_bc, preferred_element_type=jnp.float32)
    dt_pre = jnp.dot(tokens, w_dt, preferred_element_type=jnp.float32)
    values = conv_silu(x_pre, conv_x_state, conv_x_w)
    bc_conv = conv_silu(bc_pre, conv_bc_state, conv_bc_w)
    states = w_bc.shape[1] // 2
    b_mat = bc_conv[:, :states]
    c_mat = bc_conv[:, states:]
    delta = jax.nn.softplus(dt_pre + dt_bias)
    log_decay = -delta * decay_rate
    ssm, state_out = ssd_blocks(values, b_mat, c_mat, delta, log_decay, state_in, SSD_BLOCK)
    ssm = ssm + skip_d[None, :, None] * values
    gated = ssm * jax.nn.silu(gate_pre)
    square_mean = lax.optimization_barrier(jnp.mean(gated * gated, axis=2, keepdims=True))
    normed = (gated * lax.rsqrt(square_mean + 1e-05) * norm_gain).astype(jnp.bfloat16)
    mixed_out = jnp.dot(normed.reshape(total, heads * width), w_out.reshape(heads * width, model), preferred_element_type=jnp.float32).astype(jnp.bfloat16)
    return (mixed_out, state_out)
```

```python
import functools

import jax
import jax.numpy as jnp
from jax import lax
from jax.experimental import pallas as pl
from jax.experimental.pallas import tpu as pltpu
from jax.sharding import PartitionSpec as P

SSD_BLOCK = 256


def conv_silu(pre, carried, taps):
    padded = jnp.concatenate([carried, pre], axis=0)
    length = pre.shape[0]
    acc = jnp.zeros(pre.shape, jnp.float32)
    for index in range(taps.shape[0]):
        acc = acc + taps[index] * padded[index : index + length]
    return jax.nn.silu(acc)


def ssd_blocks(values, b_mat, c_mat, delta, log_decay, state, block):
    total, heads, width = values.shape
    count = total // block
    states = b_mat.shape[1]
    lower = jnp.arange(block)[:, None] >= jnp.arange(block)[None, :]
    high = lax.Precision.HIGHEST

    def advance(carry, inputs):
        vals, bm, cm, dl, ld = inputs
        cum = jnp.cumsum(ld, axis=0)
        scores = jnp.dot(cm, bm.T, precision=high)
        gap = cum.T[:, :, None] - cum.T[:, None, :]
        decay = jnp.exp(jnp.where(lower[None], gap, -jnp.inf))
        weights = decay * scores[None]
        scaled = vals * dl[:, :, None]
        inner = jnp.einsum("hts,shp->thp", weights, scaled, precision=high)
        carried = jnp.exp(cum)[:, :, None] * jnp.einsum("tn,hpn->thp", cm, carry, precision=high)
        tail = jnp.exp(cum[-1][None, :] - cum)
        update = jnp.einsum("sh,shp,sn->hpn", tail, scaled, bm, precision=high)
        new_state = jnp.exp(cum[-1])[:, None, None] * carry + update
        return (new_state, inner + carried)

    inputs = (
        values.reshape(count, block, heads, width),
        b_mat.reshape(count, block, states),
        c_mat.reshape(count, block, states),
        delta.reshape(count, block, heads),
        log_decay.reshape(count, block, heads),
    )
    final, outputs = lax.scan(advance, state, inputs)
    return (outputs.reshape(total, heads, width), final)


VM = pl.BlockSpec(memory_space=pltpu.VMEM)
HBM = pl.BlockSpec(memory_space=pl.ANY)
MESH = pl.DeviceIdType.MESH
TILE = 256


def greet(n_gx, n_gy):
    barrier = pltpu.get_barrier_semaphore()
    for axis, count in (("gx", n_gx), ("gy", n_gy)):
        me = lax.axis_index(axis)
        for step in range(1, count):
            peer = lax.rem(me + step, count)
            pl.semaphore_signal(barrier, inc=1, device_id={axis: peer}, device_id_type=MESH)
    pl.semaphore_wait(barrier, n_gx + n_gy - 2)


def remote(src, dst, send, recv, axis, peer):
    return pltpu.make_async_remote_copy(
        src_ref=src,
        dst_ref=dst,
        send_sem=send,
        recv_sem=recv,
        device_id={axis: peer},
        device_id_type=MESH,
    )


def project_kernel(
    n_gx, n_gy, heads, width,
    tok_ref, wg_ref, wx_ref, wbc_ref, wdt_ref,
    chan_ref, bc_ref, dt_ref,
    full, w, wbc, part, snd, rcv, bc_rcv, bc_full, dt_rcv,
    load_sem, gx_send, gx_recv, gy_send, gy_recv,
):
    gx, gy = lax.axis_index("gx"), lax.axis_index("gy")
    rows = tok_ref.shape[0]
    inner = heads * width
    local = width // n_gy
    loads = [
        pltpu.make_async_copy(wbc_ref, wbc, load_sem.at[0]),
        pltpu.make_async_copy(wg_ref, w.at[:, pl.ds(0, inner)], load_sem.at[1]),
        pltpu.make_async_copy(wx_ref, w.at[:, pl.ds(inner, inner)], load_sem.at[2]),
    ]
    for load in loads:
        load.start()
    greet(n_gx, n_gy)
    mine = pl.ds(pl.multiple_of(gx * rows, rows), rows)
    gathers = []
    for step in range(1, n_gx):
        peer = lax.rem(gx + step, n_gx)
        copy = remote(
            tok_ref, full.at[mine], gx_send.at[0, step], gx_recv.at[0, step], "gx", peer
        )
        copy.start()
        gathers.append(copy)
    full[mine] = tok_ref[...]
    loads[0].wait()
    bc_rcv[0] = jnp.dot(tok_ref[...], wbc[...], preferred_element_type=jnp.float32)
    bc_sums = []
    for step in range(1, n_gy):
        peer = lax.rem(gy + step, n_gy)
        copy = remote(
            bc_rcv.at[0], bc_rcv.at[step], gy_send.at[0, step], gy_recv.at[0, step], "gy", peer
        )
        copy.start()
        bc_sums.append(copy)
    for copy in bc_sums:
        copy.wait()
    bc_sum = bc_rcv[0]
    for step in range(1, n_gy):
        bc_sum = bc_sum + bc_rcv[step]
    bc_full[mine] = bc_sum
    bc_gathers = []
    for step in range(1, n_gx):
        peer = lax.rem(gx + step, n_gx)
        copy = remote(
            bc_full.at[mine], bc_full.at[mine], gx_send.at[1, step], gx_recv.at[1, step], "gx", peer
        )
        copy.start()
        bc_gathers.append(copy)
    for copy in gathers:
        copy.wait()
    dt_rcv[0] = lax.dot_general(
        wdt_ref[...], full[...], (((1,), (1,)), ((), ())), preferred_element_type=jnp.float32
    )
    dt_sums = []
    for step in range(1, n_gy):
        peer = lax.rem(gy + step, n_gy)
        copy = remote(
            dt_rcv.at[0], dt_rcv.at[step], gy_send.at[1, step], gy_recv.at[1, step], "gy", peer
        )
        copy.start()
        dt_sums.append(copy)
    loads[1].wait()
    loads[2].wait()

    def tile(index, carry):
        cols = pl.ds(pl.multiple_of(index * TILE, TILE), TILE)
        part[:, cols] = jnp.dot(full[...], w[:, cols], preferred_element_type=jnp.float32)
        return carry

    lax.fori_loop(0, 2 * inner // TILE, tile, 0)
    for owner in range(n_gy):
        pieces = [
            part[:, head * width + owner * local : head * width + (owner + 1) * local]
            for head in range(2 * heads)
        ]
        snd[owner] = jnp.concatenate(pieces, axis=1).astype(jnp.bfloat16)
    sums = []
    for step in range(1, n_gy):
        peer = lax.rem(gy + step, n_gy)
        copy = remote(
            snd.at[peer], rcv.at[step], gy_send.at[2, step], gy_recv.at[2, step], "gy", peer
        )
        copy.start()
        sums.append(copy)
    for copy in bc_gathers:
        copy.wait()
    bc_ref[...] = bc_full[...]
    for copy in dt_sums:
        copy.wait()
    dt_sum = dt_rcv[0]
    for step in range(1, n_gy):
        dt_sum = dt_sum + dt_rcv[step]
    dt_ref[...] = dt_sum
    for copy in sums:
        copy.wait()
    total = snd[gy].astype(jnp.float32)
    for step in range(1, n_gy):
        total = total + rcv[step].astype(jnp.float32)
    chan_ref[...] = total


def out_kernel(
    n_gx, n_gy, heads, width,
    gated_ref, gain_ref, w_ref, out_ref,
    whole, normed, w, prod, rcv,
    load_sem, gy_sem, gx_sem,
):
    gx, gy = lax.axis_index("gx"), lax.axis_index("gy")
    rows, out_cols = out_ref.shape
    local = width // n_gy
    load = pltpu.make_async_copy(w_ref, w, load_sem.at[0])
    load.start()
    greet(n_gx, n_gy)
    copies = []
    for step in range(1, n_gy):
        peer = lax.rem(gy + step, n_gy)
        copy = remote(
            gated_ref, whole.at[gy], gy_sem.at[0, step], gy_sem.at[1, step], "gy", peer
        )
        copy.start()
        copies.append(copy)
    whole[gy] = gated_ref[...]
    for copy in copies:
        copy.wait()
    blocks = [whole[owner].astype(jnp.float32) for owner in range(n_gy)]
    for head in range(heads):
        row = jnp.concatenate(
            [block[:, head * local : (head + 1) * local] for block in blocks], axis=1
        )
        mean = jnp.mean(row * row, axis=1, keepdims=True)
        normed[:, head * width : (head + 1) * width] = (
            row * lax.rsqrt(mean + 1e-05) * gain_ref[head : head + 1, :]
        ).astype(jnp.bfloat16)
    load.wait()

    def tile(index, carry):
        cols = pl.ds(pl.multiple_of(index * TILE, TILE), TILE)
        prod[:, cols] = jnp.dot(
            normed[...], w[:, cols], preferred_element_type=jnp.float32
        ).astype(jnp.bfloat16)
        return carry

    lax.fori_loop(0, out_cols // TILE, tile, 0)
    copies = []
    for step in range(1, n_gx):
        peer = lax.rem(gx + step, n_gx)
        theirs = pl.ds(pl.multiple_of(peer * rows, rows), rows)
        copy = remote(
            prod.at[theirs], rcv.at[step], gx_sem.at[0, step], gx_sem.at[1, step], "gx", peer
        )
        copy.start()
        copies.append(copy)
    total = prod[pl.ds(pl.multiple_of(gx * rows, rows), rows)].astype(jnp.float32)
    for step in range(1, n_gx):
        copies[step - 1].wait()
        total = total + rcv[step].astype(jnp.float32)
    out_ref[...] = total.astype(jnp.bfloat16)


def per_device(
    tokens,
    w_gate,
    w_x,
    w_bc,
    w_dt,
    conv_x_w,
    conv_bc_w,
    conv_x_state,
    conv_bc_state,
    dt_bias,
    decay_rate,
    skip_d,
    state_in,
    norm_gain,
    w_out,
):
    n_gx, n_gy = lax.axis_size("gx"), lax.axis_size("gy")
    d_rows, heads_here, head_width = w_gate.shape
    inner_here = heads_here * head_width
    states_two = w_bc.shape[1]
    rows = tokens.shape[0]
    total = rows * n_gx
    local = head_width // n_gy
    seg = heads_here * local
    channels, bc_pre, dt_pre = pl.pallas_call(
        functools.partial(project_kernel, n_gx, n_gy, heads_here, head_width),
        out_shape=(
            jax.ShapeDtypeStruct((total, 2 * seg), jnp.float32),
            jax.ShapeDtypeStruct((total, states_two), jnp.float32),
            jax.ShapeDtypeStruct((heads_here, total), jnp.float32),
        ),
        in_specs=[VM, HBM, HBM, HBM, VM],
        out_specs=(VM, VM, VM),
        scratch_shapes=[
            pltpu.VMEM((total, d_rows), jnp.bfloat16),
            pltpu.VMEM((d_rows, 2 * inner_here), jnp.bfloat16),
            pltpu.VMEM((d_rows, states_two), jnp.bfloat16),
            pltpu.VMEM((total, 2 * inner_here), jnp.float32),
            pltpu.VMEM((n_gy, total, 2 * seg), jnp.bfloat16),
            pltpu.VMEM((n_gy, total, 2 * seg), jnp.bfloat16),
            pltpu.VMEM((n_gy, rows, states_two), jnp.float32),
            pltpu.VMEM((total, states_two), jnp.float32),
            pltpu.VMEM((n_gy, heads_here, total), jnp.float32),
            pltpu.SemaphoreType.DMA((3,)),
            pltpu.SemaphoreType.DMA((2, n_gx)),
            pltpu.SemaphoreType.DMA((2, n_gx)),
            pltpu.SemaphoreType.DMA((3, n_gy)),
            pltpu.SemaphoreType.DMA((3, n_gy)),
        ],
        compiler_params=pltpu.CompilerParams(
            collective_id=0, has_side_effects=True, vmem_limit_bytes=48 * 1024 * 1024
        ),
    )(
        tokens,
        w_gate.reshape(d_rows, inner_here),
        w_x.reshape(d_rows, inner_here),
        w_bc,
        w_dt.T,
    )
    gate_pre = channels[:, :seg]
    taps = conv_x_w.shape[0]
    flat_values = conv_silu(
        channels[:, seg:], conv_x_state.reshape(taps - 1, seg), conv_x_w.reshape(taps, seg)
    )
    values = flat_values.reshape(total, heads_here, local)
    bc_conv = conv_silu(bc_pre, conv_bc_state, conv_bc_w)
    half_states = states_two // 2
    b_mat = bc_conv[:, :half_states]
    c_mat = bc_conv[:, half_states:]
    delta = jax.nn.softplus(dt_pre.T + dt_bias)
    log_decay = -delta * decay_rate
    ssm, state_out = ssd_blocks(values, b_mat, c_mat, delta, log_decay, state_in, SSD_BLOCK)
    ssm = ssm + skip_d[None, :, None] * values
    gated = (ssm.reshape(total, seg) * jax.nn.silu(gate_pre)).astype(jnp.bfloat16)
    out_cols = w_out.shape[2]
    summed = pl.pallas_call(
        functools.partial(out_kernel, n_gx, n_gy, heads_here, head_width),
        out_shape=jax.ShapeDtypeStruct((rows, out_cols), jnp.bfloat16),
        in_specs=[VM, VM, HBM],
        out_specs=VM,
        scratch_shapes=[
            pltpu.VMEM((n_gy, total, seg), jnp.bfloat16),
            pltpu.VMEM((total, inner_here), jnp.bfloat16),
            pltpu.VMEM((inner_here, out_cols), jnp.bfloat16),
            pltpu.VMEM((total, out_cols), jnp.bfloat16),
            pltpu.VMEM((n_gx, rows, out_cols), jnp.bfloat16),
            pltpu.SemaphoreType.DMA((1,)),
            pltpu.SemaphoreType.DMA((2, n_gy)),
            pltpu.SemaphoreType.DMA((2, n_gx)),
        ],
        compiler_params=pltpu.CompilerParams(
            collective_id=1, has_side_effects=True, vmem_limit_bytes=48 * 1024 * 1024
        ),
    )(gated, norm_gain, w_out.reshape(inner_here, out_cols))
    return (summed, state_out)


def solution(mesh):
    in_specs = (
        P(("groups", "gx"), "gy"),
        P("gy", "gx", None),
        P("gy", "gx", None),
        P("gy", None),
        P("gy", "gx"),
        P(None, "gx", "gy"),
        P(),
        P(None, ("groups", "gx"), "gy"),
        P(None, "groups"),
        P("gx"),
        P("gx"),
        P("gx"),
        P(("groups", "gx"), "gy", None),
        P("gx", None),
        P("gx", None, "gy"),
    )
    out_specs = (P(("groups", "gx"), "gy"), P(("groups", "gx"), "gy", None))
    return jax.shard_map(
        per_device, mesh=mesh, in_specs=in_specs, out_specs=out_specs, check_vma=False
    )
```

```python
import functools

import jax
import jax.numpy as jnp
from jax import lax
from jax.experimental import pallas as pl
from jax.experimental.pallas import tpu as pltpu
from jax.sharding import PartitionSpec as P

SSD_BLOCK = 256


def conv_silu(pre, carried, taps):
    padded = jnp.concatenate([carried, pre], axis=0)
    length = pre.shape[0]
    acc = jnp.zeros(pre.shape, jnp.float32)
    for index in range(taps.shape[0]):
        acc = acc + taps[index] * padded[index : index + length]
    return jax.nn.silu(acc)


def ssd_blocks(values, b_mat, c_mat, delta, log_decay, state, block):
    total, heads, width = values.shape
    count = total // block
    states = b_mat.shape[1]
    lower = jnp.arange(block)[:, None] >= jnp.arange(block)[None, :]
    high = lax.Precision.HIGHEST

    def advance(carry, inputs):
        vals, bm, cm, dl, ld = inputs
        cum = jnp.cumsum(ld, axis=0)
        scores = jnp.dot(cm, bm.T, precision=high)
        gap = cum.T[:, :, None] - cum.T[:, None, :]
        decay = jnp.exp(jnp.where(lower[None], gap, -jnp.inf))
        weights = decay * scores[None]
        scaled = vals * dl[:, :, None]
        inner = jnp.einsum("hts,shp->thp", weights, scaled, precision=high)
        carried = jnp.exp(cum)[:, :, None] * jnp.einsum("tn,hpn->thp", cm, carry, precision=high)
        tail = jnp.exp(cum[-1][None, :] - cum)
        update = jnp.einsum("sh,shp,sn->hpn", tail, scaled, bm, precision=high)
        new_state = jnp.exp(cum[-1])[:, None, None] * carry + update
        return (new_state, inner + carried)

    inputs = (
        values.reshape(count, block, heads, width),
        b_mat.reshape(count, block, states),
        c_mat.reshape(count, block, states),
        delta.reshape(count, block, heads),
        log_decay.reshape(count, block, heads),
    )
    final, outputs = lax.scan(advance, state, inputs)
    return (outputs.reshape(total, heads, width), final)


VM = pl.BlockSpec(memory_space=pltpu.VMEM)
HBM = pl.BlockSpec(memory_space=pl.ANY)
MESH = pl.DeviceIdType.MESH
TILE = 256
DEPTH = 128
LANES = 128
CHUNKS = 2


def greet(n_gx, n_gy):
    barrier = pltpu.get_barrier_semaphore()
    for axis, count in (("gx", n_gx), ("gy", n_gy)):
        me = lax.axis_index(axis)
        for step in range(1, count):
            peer = lax.rem(me + step, count)
            pl.semaphore_signal(barrier, inc=1, device_id={axis: peer}, device_id_type=MESH)
    pl.semaphore_wait(barrier, n_gx + n_gy - 2)


def remote(src, dst, send, recv, axis, peer):
    return pltpu.make_async_remote_copy(
        src_ref=src,
        dst_ref=dst,
        send_sem=send,
        recv_sem=recv,
        device_id={axis: peer},
        device_id_type=MESH,
    )


def project_kernel(
    n_gx, n_gy, heads, width,
    tok_ref, wg_ref, wx_ref, wbc_ref, wdt_ref,
    chan_ref, bc_ref, dt_ref,
    full, raw, w, wbc, spread, part, snd, rcv, bc_rcv, bc_full, dt_rcv,
    load_sem, gx_send, gx_recv, gy_send, gy_recv, sum_send, sum_recv,
):
    gx, gy = lax.axis_index("gx"), lax.axis_index("gy")
    rows = tok_ref.shape[0]
    depth = wg_ref.shape[0]
    local = width // n_gy
    core, chip, chips = gx % 2, gx // 2, n_gx // 2
    sibling = gx + 1 - 2 * core
    loads = [
        pltpu.make_async_copy(wbc_ref, wbc, load_sem.at[0]),
        pltpu.make_async_copy(wg_ref, raw.at[0], load_sem.at[1]),
        pltpu.make_async_copy(wx_ref, raw.at[1], load_sem.at[2]),
    ]
    for load in loads:
        load.start()
    greet(n_gx, n_gy)

    def block(index):
        return pl.ds(pl.multiple_of(index * rows, rows), rows)

    mine = block(gx)
    crossing = []
    for step in range(1, chips):
        peer = ((chip + step) % chips) * 2 + core
        copy = remote(
            tok_ref, full.at[mine], gx_send.at[0, step], gx_recv.at[0, step], "gx", peer
        )
        copy.start()
        crossing.append(copy)
    paired = [remote(tok_ref, full.at[mine], gx_send.at[0, 0], gx_recv.at[0, 0], "gx", sibling)]
    paired[0].start()
    full[mine] = tok_ref[...]
    loads[0].wait()
    bc_rcv[0] = jnp.dot(tok_ref[...], wbc[...], preferred_element_type=jnp.float32)
    bc_sums = []
    for step in range(1, n_gy):
        peer = lax.rem(gy + step, n_gy)
        copy = remote(
            bc_rcv.at[0], bc_rcv.at[step], gy_send.at[0, step], gy_recv.at[0, step], "gy", peer
        )
        copy.start()
        bc_sums.append(copy)

    def flatten(which):
        def body(index, carry):
            start = pl.multiple_of(index * DEPTH, DEPTH)
            chunk = raw[which, pl.ds(start, DEPTH)].astype(jnp.float32)
            spread[...] = chunk.reshape(DEPTH * heads, width)
            for head in range(heads):
                column = (which * heads + head) * width
                w[pl.ds(start, DEPTH), column : column + width] = spread[
                    pl.ds(head, DEPTH, stride=heads), :
                ].astype(jnp.bfloat16)
            return carry

        loads[1 + which].wait()
        lax.fori_loop(0, depth // DEPTH, body, 0)

    flatten(0)
    for step in range(1, chips):
        crossing[step - 1].wait()
        came = block(((chip + chips - step) % chips) * 2 + core)
        copy = remote(
            full.at[came], full.at[came],
            gx_send.at[0, chips + step], gx_recv.at[0, chips + step], "gx", sibling,
        )
        copy.start()
        paired.append(copy)
    for copy in bc_sums:
        copy.wait()
    bc_sum = bc_rcv[0]
    for step in range(1, n_gy):
        bc_sum = bc_sum + bc_rcv[step]
    bc_full[mine] = bc_sum
    bc_gathers = []
    for step in range(1, n_gx):
        peer = lax.rem(gx + step, n_gx)
        copy = remote(
            bc_full.at[mine], bc_full.at[mine], gx_send.at[1, step], gx_recv.at[1, step], "gx", peer
        )
        copy.start()
        bc_gathers.append(copy)
    flatten(1)
    for copy in paired:
        copy.wait()
    dt_rcv[0] = lax.dot_general(
        wdt_ref[...], full[...], (((1,), (1,)), ((), ())), preferred_element_type=jnp.float32
    )
    dt_sums = []
    for step in range(1, n_gy):
        peer = lax.rem(gy + step, n_gy)
        copy = remote(
            dt_rcv.at[0], dt_rcv.at[step], gy_send.at[1, step], gy_recv.at[1, step], "gy", peer
        )
        copy.start()
        dt_sums.append(copy)

    groups, span = snd.shape[1], part.shape[1]
    sums = []
    for group in range(groups):

        def tile(index, carry):
            into = pl.ds(pl.multiple_of(index * TILE, TILE), TILE)
            cols = pl.ds(pl.multiple_of(group * span + index * TILE, TILE), TILE)
            part[:, into] = jnp.dot(full[...], w[:, cols], preferred_element_type=jnp.float32)
            return carry

        lax.fori_loop(0, span // TILE, tile, 0)
        for owner in range(n_gy):
            pieces = [
                part[:, head * width + owner * local : head * width + (owner + 1) * local]
                for head in range(span // width)
            ]
            snd[owner, group] = jnp.concatenate(pieces, axis=1).astype(jnp.bfloat16)
        for step in range(1, n_gy):
            peer = lax.rem(gy + step, n_gy)
            copy = remote(
                snd.at[peer, group], rcv.at[step, group],
                sum_send.at[group, step], sum_recv.at[group, step], "gy", peer,
            )
            copy.start()
            sums.append(copy)
    for copy in bc_gathers:
        copy.wait()
    bc_ref[...] = bc_full[...]
    for copy in dt_sums:
        copy.wait()
    dt_sum = dt_rcv[0]
    for step in range(1, n_gy):
        dt_sum = dt_sum + dt_rcv[step]
    dt_ref[...] = dt_sum
    lanes = snd.shape[3]
    for group in range(groups):
        total = snd[gy, group].astype(jnp.float32)
        for step in range(1, n_gy):
            sums[group * (n_gy - 1) + step - 1].wait()
            total = total + rcv[step, group].astype(jnp.float32)
        chan_ref[:, group * lanes : (group + 1) * lanes] = total


def out_kernel(
    n_gx, n_gy, heads, width,
    gated_ref, gain_ref, w_ref, out_ref,
    whole, normed, w, prod, paired, mixed, rcv,
    load_sem, gy_sem, pair_sem, gx_sem,
):
    gx, gy = lax.axis_index("gx"), lax.axis_index("gy")
    rows, out_cols = out_ref.shape
    local = width // n_gy
    load = pltpu.make_async_copy(w_ref, w, load_sem.at[0])
    load.start()
    greet(n_gx, n_gy)
    copies = []
    for step in range(1, n_gy):
        peer = lax.rem(gy + step, n_gy)
        copy = remote(
            gated_ref, whole.at[gy], gy_sem.at[0, step], gy_sem.at[1, step], "gy", peer
        )
        copy.start()
        copies.append(copy)
    whole[gy] = gated_ref[...]
    for copy in copies:
        copy.wait()
    blocks = [whole[owner].astype(jnp.float32) for owner in range(n_gy)]
    for head in range(heads):
        row = jnp.concatenate(
            [block[:, head * local : (head + 1) * local] for block in blocks], axis=1
        )
        mean = jnp.mean(row * row, axis=1, keepdims=True)
        normed[:, head * width : (head + 1) * width] = (
            row * lax.rsqrt(mean + 1e-05) * gain_ref[head : head + 1, :]
        ).astype(jnp.bfloat16)
    load.wait()

    core, chip, chips = gx % 2, gx // 2, n_gx // 2
    sibling = gx + 1 - 2 * core
    span = out_cols // CHUNKS

    def block(index):
        return pl.ds(pl.multiple_of(index * rows, rows), rows)

    to_sibling = []
    for chunk in range(CHUNKS):

        def tile(index, carry):
            cols = pl.ds(pl.multiple_of(chunk * span + index * TILE, TILE), TILE)
            prod[:, cols] = jnp.dot(
                normed[...], w[:, cols], preferred_element_type=jnp.float32
            ).astype(jnp.bfloat16)
            return carry

        lax.fori_loop(0, span // TILE, tile, 0)
        cols = pl.ds(chunk * span, span)
        for step in range(chips):
            other = (chip + step) % chips
            copy = remote(
                prod.at[block(2 * other + 1 - core), cols], paired.at[step, :, cols],
                pair_sem.at[chunk, 0, step], pair_sem.at[chunk, 1, step], "gx", sibling,
            )
            copy.start()
            to_sibling.append(copy)
    copies = []
    for chunk in range(CHUNKS):
        cols = pl.ds(chunk * span, span)
        for step in range(chips):
            to_sibling[chunk * chips + step].wait()
        for step in range(1, chips):
            peer = ((chip + step) % chips) * 2 + core
            mixed[step, :, cols] = (
                prod[block(peer), cols].astype(jnp.float32)
                + paired[step, :, cols].astype(jnp.float32)
            ).astype(jnp.bfloat16)
            copy = remote(
                mixed.at[step, :, cols], rcv.at[step, :, cols],
                gx_sem.at[chunk, 0, step], gx_sem.at[chunk, 1, step], "gx", peer,
            )
            copy.start()
            copies.append(copy)
    for chunk in range(CHUNKS):
        cols = pl.ds(chunk * span, span)
        total = prod[block(gx), cols].astype(jnp.float32) + paired[0, :, cols].astype(jnp.float32)
        for step in range(1, chips):
            copies[chunk * (chips - 1) + step - 1].wait()
            total = total + rcv[step, :, cols].astype(jnp.float32)
        out_ref[:, cols] = total.astype(jnp.bfloat16)


def per_device(
    tokens,
    w_gate,
    w_x,
    w_bc,
    w_dt,
    conv_x_w,
    conv_bc_w,
    conv_x_state,
    conv_bc_state,
    dt_bias,
    decay_rate,
    skip_d,
    state_in,
    norm_gain,
    w_out,
):
    n_gx, n_gy = lax.axis_size("gx"), lax.axis_size("gy")
    d_rows, heads_here, head_width = w_gate.shape
    inner_here = heads_here * head_width
    states_two = w_bc.shape[1]
    rows = tokens.shape[0]
    total = rows * n_gx
    local = head_width // n_gy
    seg = heads_here * local
    lanes = min(LANES, 2 * seg)
    groups = 2 * seg // lanes
    channels, bc_pre, dt_pre = pl.pallas_call(
        functools.partial(project_kernel, n_gx, n_gy, heads_here, head_width),
        out_shape=(
            jax.ShapeDtypeStruct((total, 2 * seg), jnp.float32),
            jax.ShapeDtypeStruct((total, states_two), jnp.float32),
            jax.ShapeDtypeStruct((heads_here, total), jnp.float32),
        ),
        in_specs=[VM, HBM, HBM, HBM, VM],
        out_specs=(VM, VM, VM),
        scratch_shapes=[
            pltpu.VMEM((total, d_rows), jnp.bfloat16),
            pltpu.VMEM((2, d_rows, heads_here, head_width), jnp.bfloat16),
            pltpu.VMEM((d_rows, 2 * inner_here), jnp.bfloat16),
            pltpu.VMEM((d_rows, states_two), jnp.bfloat16),
            pltpu.VMEM((DEPTH * heads_here, head_width), jnp.float32),
            pltpu.VMEM((total, 2 * inner_here // groups), jnp.float32),
            pltpu.VMEM((n_gy, groups, total, lanes), jnp.bfloat16),
            pltpu.VMEM((n_gy, groups, total, lanes), jnp.bfloat16),
            pltpu.VMEM((n_gy, rows, states_two), jnp.float32),
            pltpu.VMEM((total, states_two), jnp.float32),
            pltpu.VMEM((n_gy, heads_here, total), jnp.float32),
            pltpu.SemaphoreType.DMA((3,)),
            pltpu.SemaphoreType.DMA((2, n_gx)),
            pltpu.SemaphoreType.DMA((2, n_gx)),
            pltpu.SemaphoreType.DMA((2, n_gy)),
            pltpu.SemaphoreType.DMA((2, n_gy)),
            pltpu.SemaphoreType.DMA((groups, n_gy)),
            pltpu.SemaphoreType.DMA((groups, n_gy)),
        ],
        compiler_params=pltpu.CompilerParams(
            collective_id=0, has_side_effects=True, vmem_limit_bytes=48 * 1024 * 1024
        ),
    )(
        tokens,
        w_gate,
        w_x,
        w_bc,
        w_dt.T,
    )
    gate_pre = channels[:, :seg]
    taps = conv_x_w.shape[0]
    flat_values = conv_silu(
        channels[:, seg:], conv_x_state.reshape(taps - 1, seg), conv_x_w.reshape(taps, seg)
    )
    values = flat_values.reshape(total, heads_here, local)
    bc_conv = conv_silu(bc_pre, conv_bc_state, conv_bc_w)
    half_states = states_two // 2
    b_mat = bc_conv[:, :half_states]
    c_mat = bc_conv[:, half_states:]
    delta = jax.nn.softplus(dt_pre.T + dt_bias)
    log_decay = -delta * decay_rate
    ssm, state_out = ssd_blocks(values, b_mat, c_mat, delta, log_decay, state_in, SSD_BLOCK)
    ssm = ssm + skip_d[None, :, None] * values
    gated = (ssm.reshape(total, seg) * jax.nn.silu(gate_pre)).astype(jnp.bfloat16)
    out_cols = w_out.shape[2]
    summed = pl.pallas_call(
        functools.partial(out_kernel, n_gx, n_gy, heads_here, head_width),
        out_shape=jax.ShapeDtypeStruct((rows, out_cols), jnp.bfloat16),
        in_specs=[VM, VM, HBM],
        out_specs=VM,
        scratch_shapes=[
            pltpu.VMEM((n_gy, total, seg), jnp.bfloat16),
            pltpu.VMEM((total, inner_here), jnp.bfloat16),
            pltpu.VMEM((inner_here, out_cols), jnp.bfloat16),
            pltpu.VMEM((total, out_cols), jnp.bfloat16),
            pltpu.VMEM((n_gx // 2, rows, out_cols), jnp.bfloat16),
            pltpu.VMEM((n_gx // 2, rows, out_cols), jnp.bfloat16),
            pltpu.VMEM((n_gx // 2, rows, out_cols), jnp.bfloat16),
            pltpu.SemaphoreType.DMA((1,)),
            pltpu.SemaphoreType.DMA((2, n_gy)),
            pltpu.SemaphoreType.DMA((CHUNKS, 2, n_gx // 2)),
            pltpu.SemaphoreType.DMA((CHUNKS, 2, n_gx // 2)),
        ],
        compiler_params=pltpu.CompilerParams(
            collective_id=1, has_side_effects=True, vmem_limit_bytes=48 * 1024 * 1024
        ),
    )(gated, norm_gain, w_out.reshape(inner_here, out_cols))
    return (summed, state_out)


def solution(mesh):
    in_specs = (
        P(("groups", "gx"), "gy"),
        P("gy", "gx", None),
        P("gy", "gx", None),
        P("gy", None),
        P("gy", "gx"),
        P(None, "gx", "gy"),
        P(),
        P(None, ("groups", "gx"), "gy"),
        P(None, "groups"),
        P("gx"),
        P("gx"),
        P("gx"),
        P(("groups", "gx"), "gy", None),
        P("gx", None),
        P("gx", None, "gy"),
    )
    out_specs = (P(("groups", "gx"), "gy"), P(("groups", "gx"), "gy", None))
    return jax.shard_map(
        per_device, mesh=mesh, in_specs=in_specs, out_specs=out_specs, check_vma=False
    )
```

```python
import functools

import jax
import jax.numpy as jnp
from jax import lax
from jax.experimental import pallas as pl
from jax.experimental.pallas import tpu as pltpu
from jax.sharding import PartitionSpec as P

SSD_BLOCK = 256


def conv_silu(pre, carried, taps):
    padded = jnp.concatenate([carried, pre], axis=0)
    length = pre.shape[0]
    acc = jnp.zeros(pre.shape, jnp.float32)
    for index in range(taps.shape[0]):
        acc = acc + taps[index] * padded[index : index + length]
    return jax.nn.silu(acc)


def ssd_blocks(values, b_mat, c_mat, delta, log_decay, state, block):
    total, heads, width = values.shape
    count = total // block
    states = b_mat.shape[1]
    lower = jnp.arange(block)[:, None] >= jnp.arange(block)[None, :]
    high = lax.Precision.HIGHEST

    def advance(carry, inputs):
        vals, bm, cm, dl, ld = inputs
        cum = jnp.cumsum(ld, axis=0)
        scores = jnp.dot(cm, bm.T, precision=high)
        gap = cum.T[:, :, None] - cum.T[:, None, :]
        decay = jnp.exp(jnp.where(lower[None], gap, -jnp.inf))
        weights = decay * scores[None]
        scaled = vals * dl[:, :, None]
        inner = jnp.einsum("hts,shp->thp", weights, scaled, precision=high)
        carried = jnp.exp(cum)[:, :, None] * jnp.einsum("tn,hpn->thp", cm, carry, precision=high)
        tail = jnp.exp(cum[-1][None, :] - cum)
        update = jnp.einsum("sh,shp,sn->hpn", tail, scaled, bm, precision=high)
        new_state = jnp.exp(cum[-1])[:, None, None] * carry + update
        return (new_state, inner + carried)

    inputs = (
        values.reshape(count, block, heads, width),
        b_mat.reshape(count, block, states),
        c_mat.reshape(count, block, states),
        delta.reshape(count, block, heads),
        log_decay.reshape(count, block, heads),
    )
    final, outputs = lax.scan(advance, state, inputs)
    return (outputs.reshape(total, heads, width), final)


VM = pl.BlockSpec(memory_space=pltpu.VMEM)
HBM = pl.BlockSpec(memory_space=pltpu.HBM)
MESH = pl.DeviceIdType.MESH
TILE = 256
DEPTH = 128
LANES = 128
CHUNKS = 2


def greet(n_gx, n_gy):
    barrier = pltpu.get_barrier_semaphore()
    for axis, count in (("gx", n_gx), ("gy", n_gy)):
        me = lax.axis_index(axis)
        for step in range(1, count):
            peer = lax.rem(me + step, count)
            pl.semaphore_signal(barrier, inc=1, device_id={axis: peer}, device_id_type=MESH)
    pl.semaphore_wait(barrier, n_gx + n_gy - 2)


def remote(src, dst, send, recv, axis, peer):
    return pltpu.make_async_remote_copy(
        src_ref=src,
        dst_ref=dst,
        send_sem=send,
        recv_sem=recv,
        device_id={axis: peer},
        device_id_type=MESH,
    )


def project_kernel(
    n_gx, n_gy, heads, width,
    tok_ref, wg_ref, wx_ref, wbc_ref, wdt_ref,
    chan_ref, bc_ref, dt_ref,
    full, raw, w, wbc, spread, part, snd, rcv, bc_rcv, bc_full, dt_rcv,
    load_sem, gx_send, gx_recv, gy_send, gy_recv, sum_send, sum_recv,
):
    gx, gy = lax.axis_index("gx"), lax.axis_index("gy")
    rows = tok_ref.shape[0]
    depth = wg_ref.shape[0]
    local = width // n_gy
    core, chip, chips = gx % 2, gx // 2, n_gx // 2
    sibling = gx + 1 - 2 * core
    loads = [
        pltpu.make_async_copy(wbc_ref, wbc, load_sem.at[0]),
        pltpu.make_async_copy(wg_ref, raw.at[0], load_sem.at[1]),
        pltpu.make_async_copy(wx_ref, raw.at[1], load_sem.at[2]),
    ]
    for load in loads:
        load.start()
    greet(n_gx, n_gy)

    def block(index):
        return pl.ds(pl.multiple_of(index * rows, rows), rows)

    mine = block(gx)
    crossing = []
    for step in range(1, chips):
        peer = ((chip + step) % chips) * 2 + core
        copy = remote(
            tok_ref, full.at[mine], gx_send.at[0, step], gx_recv.at[0, step], "gx", peer
        )
        copy.start()
        crossing.append(copy)
    paired = [remote(tok_ref, full.at[mine], gx_send.at[0, 0], gx_recv.at[0, 0], "gx", sibling)]
    paired[0].start()
    full[mine] = tok_ref[...]
    loads[0].wait()
    bc_rcv[0] = jnp.dot(tok_ref[...], wbc[...], preferred_element_type=jnp.float32)
    bc_sums = []
    for step in range(1, n_gy):
        peer = lax.rem(gy + step, n_gy)
        copy = remote(
            bc_rcv.at[0], bc_rcv.at[step], gy_send.at[0, step], gy_recv.at[0, step], "gy", peer
        )
        copy.start()
        bc_sums.append(copy)

    def flatten(which):
        def body(index, carry):
            start = pl.multiple_of(index * DEPTH, DEPTH)
            chunk = raw[which, pl.ds(start, DEPTH)].astype(jnp.float32)
            spread[...] = chunk.reshape(DEPTH * heads, width)
            for head in range(heads):
                column = (which * heads + head) * width
                w[pl.ds(start, DEPTH), column : column + width] = spread[
                    pl.ds(head, DEPTH, stride=heads), :
                ].astype(jnp.bfloat16)
            return carry

        loads[1 + which].wait()
        lax.fori_loop(0, depth // DEPTH, body, 0)

    flatten(0)
    for step in range(1, chips):
        crossing[step - 1].wait()
        came = block(((chip + chips - step) % chips) * 2 + core)
        copy = remote(
            full.at[came], full.at[came],
            gx_send.at[0, chips + step], gx_recv.at[0, chips + step], "gx", sibling,
        )
        copy.start()
        paired.append(copy)
    for copy in bc_sums:
        copy.wait()
    bc_sum = bc_rcv[0]
    for step in range(1, n_gy):
        bc_sum = bc_sum + bc_rcv[step]
    bc_full[mine] = bc_sum
    bc_gathers = []
    for step in range(1, n_gx):
        peer = lax.rem(gx + step, n_gx)
        copy = remote(
            bc_full.at[mine], bc_full.at[mine], gx_send.at[1, step], gx_recv.at[1, step], "gx", peer
        )
        copy.start()
        bc_gathers.append(copy)
    flatten(1)
    for copy in paired:
        copy.wait()
    dt_rcv[0] = lax.dot_general(
        wdt_ref[...], full[...], (((1,), (1,)), ((), ())), preferred_element_type=jnp.float32
    )
    dt_sums = []
    for step in range(1, n_gy):
        peer = lax.rem(gy + step, n_gy)
        copy = remote(
            dt_rcv.at[0], dt_rcv.at[step], gy_send.at[1, step], gy_recv.at[1, step], "gy", peer
        )
        copy.start()
        dt_sums.append(copy)

    groups, span = snd.shape[1], part.shape[1]
    sums = []
    for group in range(groups):

        def tile(index, carry):
            into = pl.ds(pl.multiple_of(index * TILE, TILE), TILE)
            cols = pl.ds(pl.multiple_of(group * span + index * TILE, TILE), TILE)
            part[:, into] = jnp.dot(full[...], w[:, cols], preferred_element_type=jnp.float32)
            return carry

        lax.fori_loop(0, span // TILE, tile, 0)
        for owner in range(n_gy):
            pieces = [
                part[:, head * width + owner * local : head * width + (owner + 1) * local]
                for head in range(span // width)
            ]
            snd[owner, group] = jnp.concatenate(pieces, axis=1).astype(jnp.bfloat16)
        for step in range(1, n_gy):
            peer = lax.rem(gy + step, n_gy)
            copy = remote(
                snd.at[peer, group], rcv.at[step, group],
                sum_send.at[group, step], sum_recv.at[group, step], "gy", peer,
            )
            copy.start()
            sums.append(copy)
    for copy in bc_gathers:
        copy.wait()
    bc_ref[...] = bc_full[...]
    for copy in dt_sums:
        copy.wait()
    dt_sum = dt_rcv[0]
    for step in range(1, n_gy):
        dt_sum = dt_sum + dt_rcv[step]
    dt_ref[...] = dt_sum
    lanes = snd.shape[3]
    for group in range(groups):
        total = snd[gy, group].astype(jnp.float32)
        for step in range(1, n_gy):
            sums[group * (n_gy - 1) + step - 1].wait()
            total = total + rcv[step, group].astype(jnp.float32)
        chan_ref[:, group * lanes : (group + 1) * lanes] = total


def out_kernel(
    n_gx, n_gy, heads, width,
    gated_ref, gain_ref, w_ref, out_ref,
    whole, normed, w, prod, paired, mixed, rcv,
    load_sem, gy_sem, pair_sem, gx_sem,
):
    gx, gy = lax.axis_index("gx"), lax.axis_index("gy")
    rows, out_cols = out_ref.shape
    local = width // n_gy
    load = pltpu.make_async_copy(w_ref, w, load_sem.at[0])
    load.start()
    greet(n_gx, n_gy)
    copies = []
    for step in range(1, n_gy):
        peer = lax.rem(gy + step, n_gy)
        copy = remote(
            gated_ref, whole.at[gy], gy_sem.at[0, step], gy_sem.at[1, step], "gy", peer
        )
        copy.start()
        copies.append(copy)
    whole[gy] = gated_ref[...]
    for copy in copies:
        copy.wait()
    blocks = [whole[owner].astype(jnp.float32) for owner in range(n_gy)]
    for head in range(heads):
        row = jnp.concatenate(
            [block[:, head * local : (head + 1) * local] for block in blocks], axis=1
        )
        mean = jnp.mean(row * row, axis=1, keepdims=True)
        normed[:, head * width : (head + 1) * width] = (
            row * lax.rsqrt(mean + 1e-05) * gain_ref[head : head + 1, :]
        ).astype(jnp.bfloat16)
    load.wait()

    core, chip, chips = gx % 2, gx // 2, n_gx // 2
    sibling = gx + 1 - 2 * core
    span = out_cols // CHUNKS

    def block(index):
        return pl.ds(pl.multiple_of(index * rows, rows), rows)

    to_sibling = []
    for chunk in range(CHUNKS):

        def tile(index, carry):
            cols = pl.ds(pl.multiple_of(chunk * span + index * TILE, TILE), TILE)
            prod[:, cols] = jnp.dot(
                normed[...], w[:, cols], preferred_element_type=jnp.float32
            ).astype(jnp.bfloat16)
            return carry

        lax.fori_loop(0, span // TILE, tile, 0)
        cols = pl.ds(chunk * span, span)
        for step in range(chips):
            other = (chip + step) % chips
            copy = remote(
                prod.at[block(2 * other + 1 - core), cols], paired.at[step, :, cols],
                pair_sem.at[chunk, 0, step], pair_sem.at[chunk, 1, step], "gx", sibling,
            )
            copy.start()
            to_sibling.append(copy)
    copies = []
    for chunk in range(CHUNKS):
        cols = pl.ds(chunk * span, span)
        for step in range(chips):
            to_sibling[chunk * chips + step].wait()
        for step in range(1, chips):
            peer = ((chip + step) % chips) * 2 + core
            mixed[step, :, cols] = (
                prod[block(peer), cols].astype(jnp.float32)
                + paired[step, :, cols].astype(jnp.float32)
            ).astype(jnp.bfloat16)
            copy = remote(
                mixed.at[step, :, cols], rcv.at[step, :, cols],
                gx_sem.at[chunk, 0, step], gx_sem.at[chunk, 1, step], "gx", peer,
            )
            copy.start()
            copies.append(copy)
    for chunk in range(CHUNKS):
        cols = pl.ds(chunk * span, span)
        total = prod[block(gx), cols].astype(jnp.float32) + paired[0, :, cols].astype(jnp.float32)
        for step in range(1, chips):
            copies[chunk * (chips - 1) + step - 1].wait()
            total = total + rcv[step, :, cols].astype(jnp.float32)
        out_ref[:, cols] = total.astype(jnp.bfloat16)


def per_device(
    tokens,
    w_gate,
    w_x,
    w_bc,
    w_dt,
    conv_x_w,
    conv_bc_w,
    conv_x_state,
    conv_bc_state,
    dt_bias,
    decay_rate,
    skip_d,
    state_in,
    norm_gain,
    w_out,
):
    n_gx, n_gy = lax.axis_size("gx"), lax.axis_size("gy")
    d_rows, heads_here, head_width = w_gate.shape
    inner_here = heads_here * head_width
    states_two = w_bc.shape[1]
    rows = tokens.shape[0]
    total = rows * n_gx
    local = head_width // n_gy
    seg = heads_here * local
    lanes = min(LANES, 2 * seg)
    groups = 2 * seg // lanes
    channels, bc_pre, dt_pre = pl.pallas_call(
        functools.partial(project_kernel, n_gx, n_gy, heads_here, head_width),
        out_shape=(
            jax.ShapeDtypeStruct((total, 2 * seg), jnp.float32),
            jax.ShapeDtypeStruct((total, states_two), jnp.float32),
            jax.ShapeDtypeStruct((heads_here, total), jnp.float32),
        ),
        in_specs=[VM, HBM, HBM, HBM, VM],
        out_specs=(VM, VM, VM),
        scratch_shapes=[
            pltpu.VMEM((total, d_rows), jnp.bfloat16),
            pltpu.VMEM((2, d_rows, heads_here, head_width), jnp.bfloat16),
            pltpu.VMEM((d_rows, 2 * inner_here), jnp.bfloat16),
            pltpu.VMEM((d_rows, states_two), jnp.bfloat16),
            pltpu.VMEM((DEPTH * heads_here, head_width), jnp.float32),
            pltpu.VMEM((total, 2 * inner_here // groups), jnp.float32),
            pltpu.VMEM((n_gy, groups, total, lanes), jnp.bfloat16),
            pltpu.VMEM((n_gy, groups, total, lanes), jnp.bfloat16),
            pltpu.VMEM((n_gy, rows, states_two), jnp.float32),
            pltpu.VMEM((total, states_two), jnp.float32),
            pltpu.VMEM((n_gy, heads_here, total), jnp.float32),
            pltpu.SemaphoreType.DMA((3,)),
            pltpu.SemaphoreType.DMA((2, n_gx)),
            pltpu.SemaphoreType.DMA((2, n_gx)),
            pltpu.SemaphoreType.DMA((2, n_gy)),
            pltpu.SemaphoreType.DMA((2, n_gy)),
            pltpu.SemaphoreType.DMA((groups, n_gy)),
            pltpu.SemaphoreType.DMA((groups, n_gy)),
        ],
        compiler_params=pltpu.CompilerParams(
            collective_id=0, has_side_effects=True, vmem_limit_bytes=56 * 1024 * 1024
        ),
    )(
        tokens,
        w_gate,
        w_x,
        w_bc,
        w_dt.T,
    )
    gate_pre = channels[:, :seg]
    taps = conv_x_w.shape[0]
    flat_values = conv_silu(
        channels[:, seg:], conv_x_state.reshape(taps - 1, seg), conv_x_w.reshape(taps, seg)
    )
    values = flat_values.reshape(total, heads_here, local)
    bc_conv = conv_silu(bc_pre, conv_bc_state, conv_bc_w)
    half_states = states_two // 2
    b_mat = bc_conv[:, :half_states]
    c_mat = bc_conv[:, half_states:]
    delta = jax.nn.softplus(dt_pre.T + dt_bias)
    log_decay = -delta * decay_rate
    ssm, state_out = ssd_blocks(values, b_mat, c_mat, delta, log_decay, state_in, SSD_BLOCK)
    ssm = ssm + skip_d[None, :, None] * values
    gated = (ssm.reshape(total, seg) * jax.nn.silu(gate_pre)).astype(jnp.bfloat16)
    out_cols = w_out.shape[2]
    summed = pl.pallas_call(
        functools.partial(out_kernel, n_gx, n_gy, heads_here, head_width),
        out_shape=jax.ShapeDtypeStruct((rows, out_cols), jnp.bfloat16),
        in_specs=[VM, VM, HBM],
        out_specs=VM,
        scratch_shapes=[
            pltpu.VMEM((n_gy, total, seg), jnp.bfloat16),
            pltpu.VMEM((total, inner_here), jnp.bfloat16),
            pltpu.VMEM((inner_here, out_cols), jnp.bfloat16),
            pltpu.VMEM((total, out_cols), jnp.bfloat16),
            pltpu.VMEM((n_gx // 2, rows, out_cols), jnp.bfloat16),
            pltpu.VMEM((n_gx // 2, rows, out_cols), jnp.bfloat16),
            pltpu.VMEM((n_gx // 2, rows, out_cols), jnp.bfloat16),
            pltpu.SemaphoreType.DMA((1,)),
            pltpu.SemaphoreType.DMA((2, n_gy)),
            pltpu.SemaphoreType.DMA((CHUNKS, 2, n_gx // 2)),
            pltpu.SemaphoreType.DMA((CHUNKS, 2, n_gx // 2)),
        ],
        compiler_params=pltpu.CompilerParams(
            collective_id=1, has_side_effects=True, vmem_limit_bytes=56 * 1024 * 1024
        ),
    )(gated, norm_gain, w_out.reshape(inner_here, out_cols))
    return (summed, state_out)


def solution(mesh):
    in_specs = (
        P(("groups", "gx"), "gy"),
        P("gy", "gx", None),
        P("gy", "gx", None),
        P("gy", None),
        P("gy", "gx"),
        P(None, "gx", "gy"),
        P(),
        P(None, ("groups", "gx"), "gy"),
        P(None, "groups"),
        P("gx"),
        P("gx"),
        P("gx"),
        P(("groups", "gx"), "gy", None),
        P("gx", None),
        P("gx", None, "gy"),
    )
    out_specs = (P(("groups", "gx"), "gy"), P(("groups", "gx"), "gy", None))
    return jax.shard_map(
        per_device, mesh=mesh, in_specs=in_specs, out_specs=out_specs, check_vma=False
    )
```

```python
import functools

import jax
import jax.numpy as jnp
from jax import lax
from jax.experimental import pallas as pl
from jax.experimental.pallas import tpu as pltpu
from jax.sharding import PartitionSpec as P

SSD_BLOCK = 256


def conv_silu(pre, carried, taps):
    padded = jnp.concatenate([carried, pre], axis=0)
    length = pre.shape[0]
    acc = jnp.zeros(pre.shape, jnp.float32)
    for index in range(taps.shape[0]):
        acc = acc + taps[index] * padded[index : index + length]
    return jax.nn.silu(acc)


def ssd_blocks(values, b_mat, c_mat, delta, log_decay, state, block):
    total, heads, width = values.shape
    count = total // block
    states = b_mat.shape[1]
    lower = jnp.arange(block)[:, None] >= jnp.arange(block)[None, :]
    high = lax.Precision.HIGHEST

    def advance(carry, inputs):
        vals, bm, cm, dl, ld = inputs
        cum = jnp.cumsum(ld, axis=0)
        scores = jnp.dot(cm, bm.T, precision=high)
        gap = cum.T[:, :, None] - cum.T[:, None, :]
        decay = jnp.exp(jnp.where(lower[None], gap, -jnp.inf))
        weights = decay * scores[None]
        scaled = vals * dl[:, :, None]
        inner = jnp.einsum("hts,shp->thp", weights, scaled, precision=high)
        carried = jnp.exp(cum)[:, :, None] * jnp.einsum("tn,hpn->thp", cm, carry, precision=high)
        tail = jnp.exp(cum[-1][None, :] - cum)
        update = jnp.einsum("sh,shp,sn->hpn", tail, scaled, bm, precision=high)
        new_state = jnp.exp(cum[-1])[:, None, None] * carry + update
        return (new_state, inner + carried)

    inputs = (
        values.reshape(count, block, heads, width),
        b_mat.reshape(count, block, states),
        c_mat.reshape(count, block, states),
        delta.reshape(count, block, heads),
        log_decay.reshape(count, block, heads),
    )
    final, outputs = lax.scan(advance, state, inputs)
    return (outputs.reshape(total, heads, width), final)


VM = pl.BlockSpec(memory_space=pltpu.VMEM)
HBM = pl.BlockSpec(memory_space=pltpu.HBM)
MESH = pl.DeviceIdType.MESH
TILE = 256
DEPTH = 128
LANES = 128
CHUNKS = 2


def greet(n_gx, n_gy):
    barrier = pltpu.get_barrier_semaphore()
    for axis, count in (("gx", n_gx), ("gy", n_gy)):
        me = lax.axis_index(axis)
        for step in range(1, count):
            peer = lax.rem(me + step, count)
            pl.semaphore_signal(barrier, inc=1, device_id={axis: peer}, device_id_type=MESH)
    pl.semaphore_wait(barrier, n_gx + n_gy - 2)


def remote(src, dst, send, recv, axis, peer):
    return pltpu.make_async_remote_copy(
        src_ref=src,
        dst_ref=dst,
        send_sem=send,
        recv_sem=recv,
        device_id={axis: peer},
        device_id_type=MESH,
    )


def project_kernel(
    n_gx, n_gy, heads, width,
    tok_ref, wg_ref, wx_ref, wbc_ref, wdt_ref,
    gate_ref, x_ref, bc_ref, dt_ref,
    full, raw, w, wbc, spread, part, snd, rcv, bc_rcv, bc_full, dt_rcv,
    load_sem, gx_send, gx_recv, gy_send, gy_recv, sum_send, sum_recv,
):
    gx, gy = lax.axis_index("gx"), lax.axis_index("gy")
    rows = tok_ref.shape[0]
    depth = wg_ref.shape[0]
    local = width // n_gy
    core, chip, chips = gx % 2, gx // 2, n_gx // 2
    sibling = gx + 1 - 2 * core
    loads = [
        pltpu.make_async_copy(wbc_ref, wbc, load_sem.at[0]),
        pltpu.make_async_copy(wg_ref, raw.at[0], load_sem.at[1]),
        pltpu.make_async_copy(wx_ref, raw.at[1], load_sem.at[2]),
    ]
    for load in loads:
        load.start()
    greet(n_gx, n_gy)

    def block(index):
        return pl.ds(pl.multiple_of(index * rows, rows), rows)

    mine = block(gx)
    crossing = []
    for step in range(1, chips):
        peer = ((chip + step) % chips) * 2 + core
        copy = remote(
            tok_ref, full.at[mine], gx_send.at[0, step], gx_recv.at[0, step], "gx", peer
        )
        copy.start()
        crossing.append(copy)
    paired = [remote(tok_ref, full.at[mine], gx_send.at[0, 0], gx_recv.at[0, 0], "gx", sibling)]
    paired[0].start()
    full[mine] = tok_ref[...]
    loads[0].wait()
    bc_rcv[0] = jnp.dot(tok_ref[...], wbc[...], preferred_element_type=jnp.float32)
    bc_sums = []
    for step in range(1, n_gy):
        peer = lax.rem(gy + step, n_gy)
        copy = remote(
            bc_rcv.at[0], bc_rcv.at[step], gy_send.at[0, step], gy_recv.at[0, step], "gy", peer
        )
        copy.start()
        bc_sums.append(copy)

    def flatten(which):
        def body(index, carry):
            start = pl.multiple_of(index * DEPTH, DEPTH)
            chunk = raw[which, pl.ds(start, DEPTH)].astype(jnp.float32)
            spread[...] = chunk.reshape(DEPTH * heads, width)
            for head in range(heads):
                column = (which * heads + head) * width
                w[pl.ds(start, DEPTH), column : column + width] = spread[
                    pl.ds(head, DEPTH, stride=heads), :
                ].astype(jnp.bfloat16)
            return carry

        loads[1 + which].wait()
        lax.fori_loop(0, depth // DEPTH, body, 0)

    flatten(0)
    for step in range(1, chips):
        crossing[step - 1].wait()
        came = block(((chip + chips - step) % chips) * 2 + core)
        copy = remote(
            full.at[came], full.at[came],
            gx_send.at[0, chips + step], gx_recv.at[0, chips + step], "gx", sibling,
        )
        copy.start()
        paired.append(copy)
    for copy in bc_sums:
        copy.wait()
    bc_sum = bc_rcv[0]
    for step in range(1, n_gy):
        bc_sum = bc_sum + bc_rcv[step]
    bc_full[mine] = bc_sum
    bc_gathers = []
    for step in range(1, n_gx):
        peer = lax.rem(gx + step, n_gx)
        copy = remote(
            bc_full.at[mine], bc_full.at[mine], gx_send.at[1, step], gx_recv.at[1, step], "gx", peer
        )
        copy.start()
        bc_gathers.append(copy)
    for copy in paired:
        copy.wait()
    dt_rcv[0] = lax.dot_general(
        wdt_ref[...], full[...], (((1,), (1,)), ((), ())), preferred_element_type=jnp.float32
    )
    dt_sums = []
    for step in range(1, n_gy):
        peer = lax.rem(gy + step, n_gy)
        copy = remote(
            dt_rcv.at[0], dt_rcv.at[step], gy_send.at[1, step], gy_recv.at[1, step], "gy", peer
        )
        copy.start()
        dt_sums.append(copy)

    groups, span = snd.shape[1], part.shape[1]
    sums = []
    if groups == 1:
        flatten(1)
    for group in range(groups):
        if groups > 1 and group == groups // 2:
            flatten(1)

        def tile(index, carry):
            into = pl.ds(pl.multiple_of(index * TILE, TILE), TILE)
            cols = pl.ds(pl.multiple_of(group * span + index * TILE, TILE), TILE)
            part[:, into] = jnp.dot(full[...], w[:, cols], preferred_element_type=jnp.float32)
            return carry

        lax.fori_loop(0, span // TILE, tile, 0)
        for owner in range(n_gy):
            pieces = [
                part[:, head * width + owner * local : head * width + (owner + 1) * local]
                for head in range(span // width)
            ]
            snd[owner, group] = jnp.concatenate(pieces, axis=1).astype(jnp.bfloat16)
        for step in range(1, n_gy):
            peer = lax.rem(gy + step, n_gy)
            copy = remote(
                snd.at[peer, group], rcv.at[step, group],
                sum_send.at[group, step], sum_recv.at[group, step], "gy", peer,
            )
            copy.start()
            sums.append(copy)
    for copy in bc_gathers:
        copy.wait()
    bc_ref[...] = bc_full[...]
    for copy in dt_sums:
        copy.wait()
    dt_sum = dt_rcv[0]
    for step in range(1, n_gy):
        dt_sum = dt_sum + dt_rcv[step]
    dt_ref[...] = dt_sum
    totals = []
    for group in range(groups):
        total = snd[gy, group].astype(jnp.float32)
        for step in range(1, n_gy):
            sums[group * (n_gy - 1) + step - 1].wait()
            total = total + rcv[step, group].astype(jnp.float32)
        totals.append(total)
    both = jnp.concatenate(totals, axis=1) if groups > 1 else totals[0]
    seg = heads * local
    gate_ref[...] = both[:, :seg]
    x_ref[...] = both[:, seg:]


def out_kernel(
    n_gx, n_gy, heads, width,
    gated_ref, gain_ref, w_ref, out_ref,
    whole, normed, w, prod, paired, mixed, rcv,
    load_sem, gy_sem, pair_sem, gx_sem,
):
    gx, gy = lax.axis_index("gx"), lax.axis_index("gy")
    rows, out_cols = out_ref.shape
    local = width // n_gy
    load = pltpu.make_async_copy(w_ref, w, load_sem.at[0])
    load.start()
    greet(n_gx, n_gy)
    parts = gy_sem.shape[0]
    lanes, held = heads * local // parts, heads // parts
    copies = []
    for piece in range(parts):
        for step in range(1, n_gy):
            peer = lax.rem(gy + step, n_gy)
            cols = pl.ds(piece * lanes, lanes)
            copy = remote(
                gated_ref.at[:, cols], whole.at[gy, :, cols],
                gy_sem.at[piece, 0, step], gy_sem.at[piece, 1, step], "gy", peer,
            )
            copy.start()
            copies.append(copy)
    whole[gy] = gated_ref[...]
    for piece in range(parts):
        for step in range(1, n_gy):
            copies[piece * (n_gy - 1) + step - 1].wait()
        blocks = [
            whole[owner, :, piece * lanes : (piece + 1) * lanes].astype(jnp.float32)
            for owner in range(n_gy)
        ]
        for index in range(held):
            head = piece * held + index
            row = jnp.concatenate(
                [block[:, index * local : (index + 1) * local] for block in blocks], axis=1
            )
            mean = jnp.mean(row * row, axis=1, keepdims=True)
            normed[:, head * width : (head + 1) * width] = (
                row * lax.rsqrt(mean + 1e-05) * gain_ref[head : head + 1, :]
            ).astype(jnp.bfloat16)
    load.wait()

    core, chip, chips = gx % 2, gx // 2, n_gx // 2
    sibling = gx + 1 - 2 * core
    span = out_cols // CHUNKS

    def block(index):
        return pl.ds(pl.multiple_of(index * rows, rows), rows)

    to_sibling = []
    for chunk in range(CHUNKS):

        def tile(index, carry):
            cols = pl.ds(pl.multiple_of(chunk * span + index * TILE, TILE), TILE)
            prod[:, cols] = jnp.dot(
                normed[...], w[:, cols], preferred_element_type=jnp.float32
            ).astype(jnp.bfloat16)
            return carry

        lax.fori_loop(0, span // TILE, tile, 0)
        cols = pl.ds(chunk * span, span)
        for step in range(chips):
            other = (chip + step) % chips
            copy = remote(
                prod.at[block(2 * other + 1 - core), cols], paired.at[step, :, cols],
                pair_sem.at[chunk, 0, step], pair_sem.at[chunk, 1, step], "gx", sibling,
            )
            copy.start()
            to_sibling.append(copy)
    copies = []
    for chunk in range(CHUNKS):
        cols = pl.ds(chunk * span, span)
        for step in range(chips):
            to_sibling[chunk * chips + step].wait()
        for step in range(1, chips):
            peer = ((chip + step) % chips) * 2 + core
            mixed[step, :, cols] = (
                prod[block(peer), cols].astype(jnp.float32)
                + paired[step, :, cols].astype(jnp.float32)
            ).astype(jnp.bfloat16)
            copy = remote(
                mixed.at[step, :, cols], rcv.at[step, :, cols],
                gx_sem.at[chunk, 0, step], gx_sem.at[chunk, 1, step], "gx", peer,
            )
            copy.start()
            copies.append(copy)
    for chunk in range(CHUNKS):
        cols = pl.ds(chunk * span, span)
        total = prod[block(gx), cols].astype(jnp.float32) + paired[0, :, cols].astype(jnp.float32)
        for step in range(1, chips):
            copies[chunk * (chips - 1) + step - 1].wait()
            total = total + rcv[step, :, cols].astype(jnp.float32)
        out_ref[:, cols] = total.astype(jnp.bfloat16)


def per_device(
    tokens,
    w_gate,
    w_x,
    w_bc,
    w_dt,
    conv_x_w,
    conv_bc_w,
    conv_x_state,
    conv_bc_state,
    dt_bias,
    decay_rate,
    skip_d,
    state_in,
    norm_gain,
    w_out,
):
    n_gx, n_gy = lax.axis_size("gx"), lax.axis_size("gy")
    d_rows, heads_here, head_width = w_gate.shape
    inner_here = heads_here * head_width
    states_two = w_bc.shape[1]
    rows = tokens.shape[0]
    total = rows * n_gx
    local = head_width // n_gy
    seg = heads_here * local
    lanes = min(LANES, 2 * seg)
    groups = 2 * seg // lanes
    gate_pre, x_pre, bc_pre, dt_pre = pl.pallas_call(
        functools.partial(project_kernel, n_gx, n_gy, heads_here, head_width),
        out_shape=(
            jax.ShapeDtypeStruct((total, seg), jnp.float32),
            jax.ShapeDtypeStruct((total, seg), jnp.float32),
            jax.ShapeDtypeStruct((total, states_two), jnp.float32),
            jax.ShapeDtypeStruct((heads_here, total), jnp.float32),
        ),
        in_specs=[VM, HBM, HBM, HBM, VM],
        out_specs=(VM, VM, VM, VM),
        scratch_shapes=[
            pltpu.VMEM((total, d_rows), jnp.bfloat16),
            pltpu.VMEM((2, d_rows, heads_here, head_width), jnp.bfloat16),
            pltpu.VMEM((d_rows, 2 * inner_here), jnp.bfloat16),
            pltpu.VMEM((d_rows, states_two), jnp.bfloat16),
            pltpu.VMEM((DEPTH * heads_here, head_width), jnp.float32),
            pltpu.VMEM((total, 2 * inner_here // groups), jnp.float32),
            pltpu.VMEM((n_gy, groups, total, lanes), jnp.bfloat16),
            pltpu.VMEM((n_gy, groups, total, lanes), jnp.bfloat16),
            pltpu.VMEM((n_gy, rows, states_two), jnp.float32),
            pltpu.VMEM((total, states_two), jnp.float32),
            pltpu.VMEM((n_gy, heads_here, total), jnp.float32),
            pltpu.SemaphoreType.DMA((3,)),
            pltpu.SemaphoreType.DMA((2, n_gx)),
            pltpu.SemaphoreType.DMA((2, n_gx)),
            pltpu.SemaphoreType.DMA((2, n_gy)),
            pltpu.SemaphoreType.DMA((2, n_gy)),
            pltpu.SemaphoreType.DMA((groups, n_gy)),
            pltpu.SemaphoreType.DMA((groups, n_gy)),
        ],
        compiler_params=pltpu.CompilerParams(
            collective_id=0, has_side_effects=True, vmem_limit_bytes=56 * 1024 * 1024
        ),
    )(
        tokens,
        w_gate,
        w_x,
        w_bc,
        w_dt.T,
    )
    taps = conv_x_w.shape[0]
    flat_values = conv_silu(
        x_pre, conv_x_state.reshape(taps - 1, seg), conv_x_w.reshape(taps, seg)
    )
    values = flat_values.reshape(total, heads_here, local)
    bc_conv = conv_silu(bc_pre, conv_bc_state, conv_bc_w)
    half_states = states_two // 2
    b_mat = bc_conv[:, :half_states]
    c_mat = bc_conv[:, half_states:]
    delta = jax.nn.softplus(dt_pre.T + dt_bias)
    log_decay = -delta * decay_rate
    ssm, state_out = ssd_blocks(values, b_mat, c_mat, delta, log_decay, state_in, SSD_BLOCK)
    ssm = ssm + skip_d[None, :, None] * values
    gated = (ssm.reshape(total, seg) * jax.nn.silu(gate_pre)).astype(jnp.bfloat16)
    out_cols = w_out.shape[2]
    summed = pl.pallas_call(
        functools.partial(out_kernel, n_gx, n_gy, heads_here, head_width),
        out_shape=jax.ShapeDtypeStruct((rows, out_cols), jnp.bfloat16),
        in_specs=[VM, VM, HBM],
        out_specs=VM,
        scratch_shapes=[
            pltpu.VMEM((n_gy, total, seg), jnp.bfloat16),
            pltpu.VMEM((total, inner_here), jnp.bfloat16),
            pltpu.VMEM((inner_here, out_cols), jnp.bfloat16),
            pltpu.VMEM((total, out_cols), jnp.bfloat16),
            pltpu.VMEM((n_gx // 2, rows, out_cols), jnp.bfloat16),
            pltpu.VMEM((n_gx // 2, rows, out_cols), jnp.bfloat16),
            pltpu.VMEM((n_gx // 2, rows, out_cols), jnp.bfloat16),
            pltpu.SemaphoreType.DMA((1,)),
            pltpu.SemaphoreType.DMA((max(1, seg // LANES), 2, n_gy)),
            pltpu.SemaphoreType.DMA((CHUNKS, 2, n_gx // 2)),
            pltpu.SemaphoreType.DMA((CHUNKS, 2, n_gx // 2)),
        ],
        compiler_params=pltpu.CompilerParams(
            collective_id=1, has_side_effects=True, vmem_limit_bytes=56 * 1024 * 1024
        ),
    )(gated, norm_gain, w_out.reshape(inner_here, out_cols))
    return (summed, state_out)


def solution(mesh):
    in_specs = (
        P(("groups", "gx"), "gy"),
        P("gy", "gx", None),
        P("gy", "gx", None),
        P("gy", None),
        P("gy", "gx"),
        P(None, "gx", "gy"),
        P(),
        P(None, ("groups", "gx"), "gy"),
        P(None, "groups"),
        P("gx"),
        P("gx"),
        P("gx"),
        P(("groups", "gx"), "gy", None),
        P("gx", None),
        P("gx", None, "gy"),
    )
    out_specs = (P(("groups", "gx"), "gy"), P(("groups", "gx"), "gy", None))
    return jax.shard_map(
        per_device, mesh=mesh, in_specs=in_specs, out_specs=out_specs, check_vma=False
    )
```

```python
import functools

import jax
import jax.numpy as jnp
from jax import lax
from jax.experimental import pallas as pl
from jax.experimental.pallas import tpu as pltpu
from jax.sharding import PartitionSpec as P

SSD_BLOCK = 256


def conv_silu(pre, carried, taps):
    padded = jnp.concatenate([carried, pre], axis=0)
    length = pre.shape[0]
    acc = jnp.zeros(pre.shape, jnp.float32)
    for index in range(taps.shape[0]):
        acc = acc + taps[index] * padded[index : index + length]
    return jax.nn.silu(acc)


def ssd_blocks(values, b_mat, c_mat, delta, log_decay, state, block):
    total, heads, width = values.shape
    count = total // block
    states = b_mat.shape[1]
    lower = jnp.arange(block)[:, None] >= jnp.arange(block)[None, :]
    high = lax.Precision.HIGHEST

    def advance(carry, inputs):
        vals, bm, cm, dl, ld = inputs
        cum = jnp.cumsum(ld, axis=0)
        scores = jnp.dot(cm, bm.T, precision=high)
        gap = cum.T[:, :, None] - cum.T[:, None, :]
        decay = jnp.exp(jnp.where(lower[None], gap, -jnp.inf))
        weights = decay * scores[None]
        scaled = vals * dl[:, :, None]
        inner = jnp.einsum("hts,shp->thp", weights, scaled)
        carried = jnp.exp(cum)[:, :, None] * jnp.einsum("tn,hpn->thp", cm, carry)
        tail = jnp.exp(cum[-1][None, :] - cum)
        update = jnp.einsum("sh,shp,sn->hpn", tail, scaled, bm)
        new_state = jnp.exp(cum[-1])[:, None, None] * carry + update
        return (new_state, inner + carried)

    inputs = (
        values.reshape(count, block, heads, width),
        b_mat.reshape(count, block, states),
        c_mat.reshape(count, block, states),
        delta.reshape(count, block, heads),
        log_decay.reshape(count, block, heads),
    )
    final, outputs = lax.scan(advance, state, inputs)
    return (outputs.reshape(total, heads, width), final)


VM = pl.BlockSpec(memory_space=pltpu.VMEM)
HBM = pl.BlockSpec(memory_space=pltpu.HBM)
MESH = pl.DeviceIdType.MESH
TILE = 256
DEPTH = 128
LANES = 128
CHUNKS = 2


def greet(n_gx, n_gy):
    barrier = pltpu.get_barrier_semaphore()
    for axis, count in (("gx", n_gx), ("gy", n_gy)):
        me = lax.axis_index(axis)
        for step in range(1, count):
            peer = lax.rem(me + step, count)
            pl.semaphore_signal(barrier, inc=1, device_id={axis: peer}, device_id_type=MESH)
    pl.semaphore_wait(barrier, n_gx + n_gy - 2)


def remote(src, dst, send, recv, axis, peer):
    return pltpu.make_async_remote_copy(
        src_ref=src,
        dst_ref=dst,
        send_sem=send,
        recv_sem=recv,
        device_id={axis: peer},
        device_id_type=MESH,
    )


def project_kernel(
    n_gx, n_gy, heads, width,
    tok_ref, wg_ref, wx_ref, wbc_ref, wdt_ref,
    gate_ref, x_ref, bc_ref, dt_ref,
    full, raw, w, wbc, spread, part, snd, rcv, bc_rcv, bc_full, dt_rcv,
    load_sem, gx_send, gx_recv, gy_send, gy_recv, sum_send, sum_recv,
):
    gx, gy = lax.axis_index("gx"), lax.axis_index("gy")
    rows = tok_ref.shape[0]
    depth = wg_ref.shape[0]
    local = width // n_gy
    core, chip, chips = gx % 2, gx // 2, n_gx // 2
    sibling = gx + 1 - 2 * core
    loads = [
        pltpu.make_async_copy(wbc_ref, wbc, load_sem.at[0]),
        pltpu.make_async_copy(wg_ref, raw.at[0], load_sem.at[1]),
        pltpu.make_async_copy(wx_ref, raw.at[1], load_sem.at[2]),
    ]
    for load in loads:
        load.start()
    greet(n_gx, n_gy)

    def block(index):
        return pl.ds(pl.multiple_of(index * rows, rows), rows)

    mine = block(gx)
    crossing = []
    for step in range(1, chips):
        peer = ((chip + step) % chips) * 2 + core
        copy = remote(
            tok_ref, full.at[mine], gx_send.at[0, step], gx_recv.at[0, step], "gx", peer
        )
        copy.start()
        crossing.append(copy)
    paired = [remote(tok_ref, full.at[mine], gx_send.at[0, 0], gx_recv.at[0, 0], "gx", sibling)]
    paired[0].start()
    full[mine] = tok_ref[...]
    loads[0].wait()
    bc_rcv[0] = jnp.dot(tok_ref[...], wbc[...], preferred_element_type=jnp.float32)
    bc_sums = []
    for step in range(1, n_gy):
        peer = lax.rem(gy + step, n_gy)
        copy = remote(
            bc_rcv.at[0], bc_rcv.at[step], gy_send.at[0, step], gy_recv.at[0, step], "gy", peer
        )
        copy.start()
        bc_sums.append(copy)

    def flatten(which):
        def body(index, carry):
            start = pl.multiple_of(index * DEPTH, DEPTH)
            chunk = raw[which, pl.ds(start, DEPTH)].astype(jnp.float32)
            spread[...] = chunk.reshape(DEPTH * heads, width)
            for head in range(heads):
                column = (which * heads + head) * width
                w[pl.ds(start, DEPTH), column : column + width] = spread[
                    pl.ds(head, DEPTH, stride=heads), :
                ].astype(jnp.bfloat16)
            return carry

        loads[1 + which].wait()
        lax.fori_loop(0, depth // DEPTH, body, 0)

    flatten(0)
    for step in range(1, chips):
        crossing[step - 1].wait()
        came = block(((chip + chips - step) % chips) * 2 + core)
        copy = remote(
            full.at[came], full.at[came],
            gx_send.at[0, chips + step], gx_recv.at[0, chips + step], "gx", sibling,
        )
        copy.start()
        paired.append(copy)
    for copy in bc_sums:
        copy.wait()
    bc_sum = bc_rcv[0]
    for step in range(1, n_gy):
        bc_sum = bc_sum + bc_rcv[step]
    bc_full[mine] = bc_sum
    bc_gathers = []
    for step in range(1, n_gx):
        peer = lax.rem(gx + step, n_gx)
        copy = remote(
            bc_full.at[mine], bc_full.at[mine], gx_send.at[1, step], gx_recv.at[1, step], "gx", peer
        )
        copy.start()
        bc_gathers.append(copy)
    for copy in paired:
        copy.wait()
    dt_rcv[0] = lax.dot_general(
        wdt_ref[...], full[...], (((1,), (1,)), ((), ())), preferred_element_type=jnp.float32
    )
    dt_sums = []
    for step in range(1, n_gy):
        peer = lax.rem(gy + step, n_gy)
        copy = remote(
            dt_rcv.at[0], dt_rcv.at[step], gy_send.at[1, step], gy_recv.at[1, step], "gy", peer
        )
        copy.start()
        dt_sums.append(copy)

    groups, span = snd.shape[1], part.shape[1]
    sums = []
    if groups == 1:
        flatten(1)
    for group in range(groups):
        if groups > 1 and group == groups // 2:
            flatten(1)

        def tile(index, carry):
            into = pl.ds(pl.multiple_of(index * TILE, TILE), TILE)
            cols = pl.ds(pl.multiple_of(group * span + index * TILE, TILE), TILE)
            part[:, into] = jnp.dot(full[...], w[:, cols], preferred_element_type=jnp.float32)
            return carry

        lax.fori_loop(0, span // TILE, tile, 0)
        for owner in range(n_gy):
            pieces = [
                part[:, head * width + owner * local : head * width + (owner + 1) * local]
                for head in range(span // width)
            ]
            snd[owner, group] = jnp.concatenate(pieces, axis=1).astype(jnp.bfloat16)
        for step in range(1, n_gy):
            peer = lax.rem(gy + step, n_gy)
            copy = remote(
                snd.at[peer, group], rcv.at[step, group],
                sum_send.at[group, step], sum_recv.at[group, step], "gy", peer,
            )
            copy.start()
            sums.append(copy)
    for copy in bc_gathers:
        copy.wait()
    bc_ref[...] = bc_full[...]
    for copy in dt_sums:
        copy.wait()
    dt_sum = dt_rcv[0]
    for step in range(1, n_gy):
        dt_sum = dt_sum + dt_rcv[step]
    dt_ref[...] = dt_sum
    totals = []
    for group in range(groups):
        total = snd[gy, group].astype(jnp.float32)
        for step in range(1, n_gy):
            sums[group * (n_gy - 1) + step - 1].wait()
            total = total + rcv[step, group].astype(jnp.float32)
        totals.append(total)
    both = jnp.concatenate(totals, axis=1) if groups > 1 else totals[0]
    seg = heads * local
    gate_ref[...] = both[:, :seg]
    x_ref[...] = both[:, seg:]


def out_kernel(
    n_gx, n_gy, heads, width,
    gated_ref, gain_ref, w_ref, out_ref,
    whole, normed, w, prod, paired, mixed, rcv,
    load_sem, gy_sem, pair_sem, gx_sem,
):
    gx, gy = lax.axis_index("gx"), lax.axis_index("gy")
    rows, out_cols = out_ref.shape
    local = width // n_gy
    load = pltpu.make_async_copy(w_ref, w, load_sem.at[0])
    load.start()
    greet(n_gx, n_gy)
    parts = gy_sem.shape[0]
    lanes, held = heads * local // parts, heads // parts
    copies = []
    for piece in range(parts):
        for step in range(1, n_gy):
            peer = lax.rem(gy + step, n_gy)
            cols = pl.ds(piece * lanes, lanes)
            copy = remote(
                gated_ref.at[:, cols], whole.at[gy, :, cols],
                gy_sem.at[piece, 0, step], gy_sem.at[piece, 1, step], "gy", peer,
            )
            copy.start()
            copies.append(copy)
    whole[gy] = gated_ref[...]
    for piece in range(parts):
        for step in range(1, n_gy):
            copies[piece * (n_gy - 1) + step - 1].wait()
        blocks = [
            whole[owner, :, piece * lanes : (piece + 1) * lanes].astype(jnp.float32)
            for owner in range(n_gy)
        ]
        for index in range(held):
            head = piece * held + index
            row = jnp.concatenate(
                [block[:, index * local : (index + 1) * local] for block in blocks], axis=1
            )
            mean = jnp.mean(row * row, axis=1, keepdims=True)
            normed[:, head * width : (head + 1) * width] = (
                row * lax.rsqrt(mean + 1e-05) * gain_ref[head : head + 1, :]
            ).astype(jnp.bfloat16)
    load.wait()

    core, chip, chips = gx % 2, gx // 2, n_gx // 2
    sibling = gx + 1 - 2 * core
    span = out_cols // CHUNKS

    def block(index):
        return pl.ds(pl.multiple_of(index * rows, rows), rows)

    to_sibling = []
    for chunk in range(CHUNKS):

        def tile(index, carry):
            cols = pl.ds(pl.multiple_of(chunk * span + index * TILE, TILE), TILE)
            prod[:, cols] = jnp.dot(
                normed[...], w[:, cols], preferred_element_type=jnp.float32
            ).astype(jnp.bfloat16)
            return carry

        lax.fori_loop(0, span // TILE, tile, 0)
        cols = pl.ds(chunk * span, span)
        for step in range(chips):
            other = (chip + step) % chips
            copy = remote(
                prod.at[block(2 * other + 1 - core), cols], paired.at[step, :, cols],
                pair_sem.at[chunk, 0, step], pair_sem.at[chunk, 1, step], "gx", sibling,
            )
            copy.start()
            to_sibling.append(copy)
    copies = []
    for chunk in range(CHUNKS):
        cols = pl.ds(chunk * span, span)
        for step in range(chips):
            to_sibling[chunk * chips + step].wait()
        for step in range(1, chips):
            peer = ((chip + step) % chips) * 2 + core
            mixed[step, :, cols] = (
                prod[block(peer), cols].astype(jnp.float32)
                + paired[step, :, cols].astype(jnp.float32)
            ).astype(jnp.bfloat16)
            copy = remote(
                mixed.at[step, :, cols], rcv.at[step, :, cols],
                gx_sem.at[chunk, 0, step], gx_sem.at[chunk, 1, step], "gx", peer,
            )
            copy.start()
            copies.append(copy)
    for chunk in range(CHUNKS):
        cols = pl.ds(chunk * span, span)
        total = prod[block(gx), cols].astype(jnp.float32) + paired[0, :, cols].astype(jnp.float32)
        for step in range(1, chips):
            copies[chunk * (chips - 1) + step - 1].wait()
            total = total + rcv[step, :, cols].astype(jnp.float32)
        out_ref[:, cols] = total.astype(jnp.bfloat16)


def per_device(
    tokens,
    w_gate,
    w_x,
    w_bc,
    w_dt,
    conv_x_w,
    conv_bc_w,
    conv_x_state,
    conv_bc_state,
    dt_bias,
    decay_rate,
    skip_d,
    state_in,
    norm_gain,
    w_out,
):
    n_gx, n_gy = lax.axis_size("gx"), lax.axis_size("gy")
    d_rows, heads_here, head_width = w_gate.shape
    inner_here = heads_here * head_width
    states_two = w_bc.shape[1]
    rows = tokens.shape[0]
    total = rows * n_gx
    local = head_width // n_gy
    seg = heads_here * local
    lanes = min(LANES, 2 * seg)
    groups = 2 * seg // lanes
    gate_pre, x_pre, bc_pre, dt_pre = pl.pallas_call(
        functools.partial(project_kernel, n_gx, n_gy, heads_here, head_width),
        out_shape=(
            jax.ShapeDtypeStruct((total, seg), jnp.float32),
            jax.ShapeDtypeStruct((total, seg), jnp.float32),
            jax.ShapeDtypeStruct((total, states_two), jnp.float32),
            jax.ShapeDtypeStruct((heads_here, total), jnp.float32),
        ),
        in_specs=[VM, HBM, HBM, HBM, VM],
        out_specs=(VM, VM, VM, VM),
        scratch_shapes=[
            pltpu.VMEM((total, d_rows), jnp.bfloat16),
            pltpu.VMEM((2, d_rows, heads_here, head_width), jnp.bfloat16),
            pltpu.VMEM((d_rows, 2 * inner_here), jnp.bfloat16),
            pltpu.VMEM((d_rows, states_two), jnp.bfloat16),
            pltpu.VMEM((DEPTH * heads_here, head_width), jnp.float32),
            pltpu.VMEM((total, 2 * inner_here // groups), jnp.float32),
            pltpu.VMEM((n_gy, groups, total, lanes), jnp.bfloat16),
            pltpu.VMEM((n_gy, groups, total, lanes), jnp.bfloat16),
            pltpu.VMEM((n_gy, rows, states_two), jnp.float32),
            pltpu.VMEM((total, states_two), jnp.float32),
            pltpu.VMEM((n_gy, heads_here, total), jnp.float32),
            pltpu.SemaphoreType.DMA((3,)),
            pltpu.SemaphoreType.DMA((2, n_gx)),
            pltpu.SemaphoreType.DMA((2, n_gx)),
            pltpu.SemaphoreType.DMA((2, n_gy)),
            pltpu.SemaphoreType.DMA((2, n_gy)),
            pltpu.SemaphoreType.DMA((groups, n_gy)),
            pltpu.SemaphoreType.DMA((groups, n_gy)),
        ],
        compiler_params=pltpu.CompilerParams(
            collective_id=0, has_side_effects=True, vmem_limit_bytes=56 * 1024 * 1024
        ),
    )(
        tokens,
        w_gate,
        w_x,
        w_bc,
        w_dt.T,
    )
    taps = conv_x_w.shape[0]
    flat_values = conv_silu(
        x_pre, conv_x_state.reshape(taps - 1, seg), conv_x_w.reshape(taps, seg)
    )
    values = flat_values.reshape(total, heads_here, local)
    bc_conv = conv_silu(bc_pre, conv_bc_state, conv_bc_w)
    half_states = states_two // 2
    b_mat = bc_conv[:, :half_states]
    c_mat = bc_conv[:, half_states:]
    delta = jax.nn.softplus(dt_pre.T + dt_bias)
    log_decay = -delta * decay_rate
    ssm, state_out = ssd_blocks(values, b_mat, c_mat, delta, log_decay, state_in, SSD_BLOCK)
    ssm = ssm + skip_d[None, :, None] * values
    gated = (ssm.reshape(total, seg) * jax.nn.silu(gate_pre)).astype(jnp.bfloat16)
    out_cols = w_out.shape[2]
    summed = pl.pallas_call(
        functools.partial(out_kernel, n_gx, n_gy, heads_here, head_width),
        out_shape=jax.ShapeDtypeStruct((rows, out_cols), jnp.bfloat16),
        in_specs=[VM, VM, HBM],
        out_specs=VM,
        scratch_shapes=[
            pltpu.VMEM((n_gy, total, seg), jnp.bfloat16),
            pltpu.VMEM((total, inner_here), jnp.bfloat16),
            pltpu.VMEM((inner_here, out_cols), jnp.bfloat16),
            pltpu.VMEM((total, out_cols), jnp.bfloat16),
            pltpu.VMEM((n_gx // 2, rows, out_cols), jnp.bfloat16),
            pltpu.VMEM((n_gx // 2, rows, out_cols), jnp.bfloat16),
            pltpu.VMEM((n_gx // 2, rows, out_cols), jnp.bfloat16),
            pltpu.SemaphoreType.DMA((1,)),
            pltpu.SemaphoreType.DMA((max(1, seg // LANES), 2, n_gy)),
            pltpu.SemaphoreType.DMA((CHUNKS, 2, n_gx // 2)),
            pltpu.SemaphoreType.DMA((CHUNKS, 2, n_gx // 2)),
        ],
        compiler_params=pltpu.CompilerParams(
            collective_id=1, has_side_effects=True, vmem_limit_bytes=56 * 1024 * 1024
        ),
    )(gated, norm_gain, w_out.reshape(inner_here, out_cols))
    return (summed, state_out)


def solution(mesh):
    in_specs = (
        P(("groups", "gx"), "gy"),
        P("gy", "gx", None),
        P("gy", "gx", None),
        P("gy", None),
        P("gy", "gx"),
        P(None, "gx", "gy"),
        P(),
        P(None, ("groups", "gx"), "gy"),
        P(None, "groups"),
        P("gx"),
        P("gx"),
        P("gx"),
        P(("groups", "gx"), "gy", None),
        P("gx", None),
        P("gx", None, "gy"),
    )
    out_specs = (P(("groups", "gx"), "gy"), P(("groups", "gx"), "gy", None))
    return jax.shard_map(
        per_device, mesh=mesh, in_specs=in_specs, out_specs=out_specs, check_vma=False
    )
```
